32 devices in a mesh: planes: 8 (over z, x), rows: 4 (over y, core).
Axes of the slice: x: 2, y: 2, z: 4, core: 2. Of those that a mesh axis runs over, the one named last changes fastest.
Arguments:
- movie: bfloat16 [65536, 2048], P(('planes', 'rows')), may hold values from -6 to 6
- entry_tile: int32 [65536], P(('planes', 'rows')), may hold values from 0 to 2047
- entry_neuron: int32 [65536], P(('planes', 'rows')), may hold values from 0 to 24575, as said below
- entry_weights: bfloat16 [65536, 128], P(('planes', 'rows')), may hold values from 0 to 0.1796875
- intersection_self: float32 [24576, 768], P(('planes', 'rows'))
- intersection_prev: float32 [24576, 768], P(('planes', 'rows')), may hold values from -0.0625 to 0.0625
- intersection_next: float32 [24576, 768], P(('planes', 'rows')), may hold values from -0.0625 to 0.0625
- prev_traces: float32 [16, 24576], P(None, ('planes', 'rows')), may hold values from 0 to 2
Outputs:
- traces: float32 [16, 24576], P(None, ('planes', 'rows'))
The draws below stay inside these ranges and needn't reach their ends.
Inputs may be any that keep to these rules, and one draw needn't show every extreme that they name: `entry_neuron`: the footprint tiles of one device come in groups of 128 consecutive entries; all entries of one group name neurons of one neuron block (neuron // 768); the first group of each device names the device's own block, and the groups of one device name distinct blocks.
All inputs are finite; a program needn't handle non-finite values.
Results may differ from the reference program's by a relative error of at most 0.0003.
Values sent between devices are 32-bit elements; how exact they have to be, the bound alone decides.
A program may use at most 192 MiB of HBM per device.

```python
import jax
import jax.numpy as jnp
from jax import lax

FRAMES = 16
TILE_VOX = 128
TILE_DEV = 2048
ENT_DEV = 2048
NEUR_DEV = 768
SWEEPS = 3
TILES = 65536
ENTRIES = 65536
NEUR = 24576
CAP = 128
N_PLANES = 8
N_ROWS = 4


def draw_entry_neuron(key, part):
    devices = NEUR // NEUR_DEV
    groups = ENT_DEV // CAP

    def one_device(owner):
        order = jax.random.permutation(jax.random.fold_in(key, owner), devices - 1)
        others = (owner + 1 + order) % devices
        return jnp.concatenate([owner[None], others[:groups - 1]])
    owners = jnp.arange(devices, dtype=jnp.int32)
    targets = jax.vmap(one_device)(owners)
    inside = jax.random.randint(jax.random.fold_in(key, 7777), (devices, groups, CAP), 0, NEUR_DEV)
    neurons = targets[:, :, None] * NEUR_DEV + inside
    return neurons.reshape(ENTRIES).astype(jnp.int32)


def draw_intersection_self(key, part):
    spread = (12.0 * NEUR_DEV) ** (-0.5)
    key_off, key_diag = jax.random.split(key)
    off = jax.random.normal(key_off, (NEUR, NEUR_DEV), jnp.float32) * spread
    own = jax.random.uniform(key_diag, (NEUR, NEUR_DEV), jnp.float32, 1.0, 1.8)
    row_index = jnp.arange(NEUR, dtype=jnp.int32)[:, None] % NEUR_DEV
    col_index = jnp.arange(NEUR_DEV, dtype=jnp.int32)[None, :]
    return jnp.where(row_index == col_index, own, off).astype(jnp.float32)


def set_ends(entries, rng, smallest, top_value):
    longest = entries.shape.index(max(entries.shape))
    spots = []
    for shift in (0, 1):
        where = [jax.random.randint(jax.random.fold_in(rng, axis), (), 0, length) for axis, length in enumerate(entries.shape)]
        where[longest] = (where[longest] + shift) % entries.shape[longest]
        spots.append(tuple(where))
    return entries.at[spots[0]].set(smallest).at[spots[1]].set(top_value)


def block_levels(own_key, shape, cuts, least, largest):
    loudness = 1.0
    for position, parts in cuts:
        draws = jax.random.uniform(jax.random.fold_in(jax.random.fold_in(own_key, 6), position), (parts,), jnp.float32, least / len(cuts), largest / len(cuts))
        loudness = loudness * jnp.repeat(jnp.exp(draws), shape[position] // parts).reshape((-1,) + (1,) * (len(shape) - 1 - position))
    return loudness


def gaussian(own_key, extent, scale, most, shards=(), kind=jnp.bfloat16):
    array = jax.random.normal(own_key, extent, jnp.float32) * scale
    if len(shards) > 0:
        array = block_levels(own_key, extent, shards, -0.22, 0.18) * array
    return jnp.clip(array, min=-most, max=most).astype(kind)


def setup_inputs(seed: int = 0) -> dict:
    key_list = jax.random.split(jax.random.key(seed), 9)
    movie = gaussian(key_list[0], (TILES, FRAMES * TILE_VOX), 1.0, 6.0, ((0, 32),))
    entry_tile = set_ends(jax.random.randint(key_list[1], (ENTRIES,), 0, TILE_DEV), jax.random.fold_in(key_list[1], 1), 0, TILE_DEV - 1).astype(jnp.int32)
    entry_neuron = draw_entry_neuron(jax.random.fold_in(key_list[8], 71), 0)
    entry_weights = jnp.clip(0.1796875 * jax.random.uniform(key_list[3], (ENTRIES, TILE_VOX), jnp.float32) ** block_levels(key_list[3], (ENTRIES, TILE_VOX), ((0, 32),), -0.2, 0.2), 0.0, 0.1796875).astype(jnp.bfloat16)
    intersection_self = draw_intersection_self(jax.random.fold_in(key_list[8], 71), 0)
    intersection_prev = gaussian(key_list[5], (NEUR, NEUR_DEV), (12 * NEUR_DEV) ** -0.5, 0.0625, ((0, 32),), jnp.float32)
    intersection_next = gaussian(key_list[6], (NEUR, NEUR_DEV), (12 * NEUR_DEV) ** -0.5, 0.0625, ((0, 32),), jnp.float32)
    prev_traces = jnp.clip(2.0 * jax.random.uniform(key_list[7], (FRAMES, NEUR), jnp.float32) ** block_levels(key_list[7], (FRAMES, NEUR), ((1, 32),), -0.2, 0.2), 0.0, 2.0)
    return {"movie": movie, "entry_tile": entry_tile, "entry_neuron": entry_neuron, "entry_weights": entry_weights, "intersection_self": intersection_self, "intersection_prev": intersection_prev, "intersection_next": intersection_next, "prev_traces": prev_traces}


def reference(movie, entry_tile, entry_neuron, entry_weights, intersection_self, intersection_prev, intersection_next, prev_traces):
    devices = N_PLANES * N_ROWS
    slabs = movie.reshape(devices, TILE_DEV, FRAMES * TILE_VOX)
    tiles_of = entry_tile.reshape(devices, ENT_DEV)
    weights_of = entry_weights.reshape(devices, ENT_DEV, TILE_VOX)

    def one_device(packed):
        slab, tiles, weights = packed
        picked = slab[tiles].reshape(ENT_DEV, FRAMES, TILE_VOX).astype(jnp.float32)
        return jnp.einsum("efv,ev->ef", picked, weights.astype(jnp.float32))

    contrib = lax.map(one_device, (slabs, tiles_of, weights_of)).reshape(ENTRIES, FRAMES)
    projected = jnp.zeros((NEUR, FRAMES), jnp.float32).at[entry_neuron].add(contrib).T
    self_blocks = intersection_self.reshape(devices, NEUR_DEV, NEUR_DEV)
    prev_blocks = intersection_prev.reshape(devices, NEUR_DEV, NEUR_DEV)
    next_blocks = intersection_next.reshape(devices, NEUR_DEV, NEUR_DEV)
    diagonal = jnp.diagonal(self_blocks, axis1=1, axis2=2).reshape(NEUR)
    hp = lax.Precision.HIGHEST
    current = prev_traces
    for sweep in range(SWEEPS):
        blocks = current.reshape(FRAMES, devices, NEUR_DEV)
        empty = jnp.zeros_like(blocks[:, :1])
        before = jnp.concatenate([empty, blocks[:, :-1]], axis=1)
        after = jnp.concatenate([blocks[:, 1:], empty], axis=1)
        coupled = jnp.einsum("fdj,dji->fdi", blocks, self_blocks, precision=hp)
        coupled = coupled + jnp.einsum("fdj,dji->fdi", before, prev_blocks, precision=hp)
        coupled = coupled + jnp.einsum("fdj,dji->fdi", after, next_blocks, precision=hp)
        coupled = coupled.reshape(FRAMES, NEUR)
        current = jnp.maximum(current + (projected - coupled) / diagonal, 0.0)
    return current
```

```python
import functools

import jax
import jax.numpy as jnp
from jax import lax
from jax.experimental import pallas as pl
from jax.experimental.pallas import tpu as pltpu
from jax.sharding import PartitionSpec as P

SWEEPS = 3
LANES = 128
STEPS = 8
BATCH = 8
F32 = jnp.float32
BF16 = jnp.bfloat16
MESH = pl.DeviceIdType.MESH
NT = (((1,), (1,)), ((), ()))


def contrib_kernel(cap, neur_dev, tile_s, neuron_s, movie, weights, neuron_v, out, staged):
    step = pl.program_id(0)
    rows = movie.shape[0]
    frames = out.shape[1] - 1

    @pl.loop(0, rows // 16)
    def _(r):
        base = pl.multiple_of(r * 16, 16)
        for f in range(frames):
            x = movie[pl.ds(base, 16), f * LANES:(f + 1) * LANES].astype(F32)
            staged[pl.ds((step * rows + base) * frames + f, 16, stride=frames), :] = x

    @pl.when(step == pl.num_programs(0) - 1)
    def _():
        for d in range(out.shape[0]):
            out[d, :frames] = jnp.zeros((frames, LANES), F32)
            out[d, frames:] = jnp.full((1, LANES), -1.0, F32)
        lane = lax.broadcasted_iota(jnp.int32, (frames, LANES), 1)
        part = 32

        @pl.loop(0, weights.shape[0] // LANES)
        def _(c):
            first = pl.multiple_of(c * LANES, LANES)
            w = weights[pl.ds(first, LANES), :]
            acc = jnp.zeros((frames, LANES), F32)
            for p in range(0, LANES, part):
                picked = [
                    staged[pl.ds(pl.multiple_of(tile_s[first + p + i] * frames, frames), frames), :].astype(BF16)
                    for i in range(part)
                ]
                prod = lax.dot_general(jnp.concatenate(picked, axis=0), w, NT, preferred_element_type=F32)
                for i in range(part):
                    acc = jnp.where(lane == p + i, prod[i * frames:(i + 1) * frames], acc)
            names = neuron_v[pl.ds(c, 1), :].astype(F32)
            for q in range(0, LANES, cap):
                owner = neuron_s[first + q] // neur_dev
                out[owner, :frames] = acc
                out[owner, frames:] = names


def halves(x):
    hi = x.astype(BF16)
    return hi, (x - hi.astype(F32)).astype(BF16)


def sweep_kernel(
    n,
    n_rows,
    slots,
    self_h,
    prev_h,
    next_h,
    start,
    traces,
    landed,
    raw,
    high,
    low,
    diag,
    projected,
    current,
    before,
    after,
    raw_sem,
    own_sem,
    send_sem,
    recv_sem,
    near_send,
    near_recv,
):
    me = lax.axis_index("planes") * n_rows + lax.axis_index("rows")
    frames, neur_dev = start.shape

    def place(d):
        return (d // n_rows, lax.rem(d, n_rows))

    loads = [pltpu.make_async_copy(h, raw.at[i], raw_sem.at[i]) for i, h in enumerate((self_h, prev_h, next_h))]
    for load in loads:
        load.start()
    own = pltpu.make_async_copy(slots.at[me], landed.at[me], own_sem)
    own.start()

    barrier = pltpu.get_barrier_semaphore()

    @pl.loop(1, n)
    def _(off):
        pl.semaphore_signal(barrier, inc=1, device_id=place(lax.rem(me + off, n)), device_id_type=MESH)

    pl.semaphore_wait(barrier, n - 1)

    def to_next(src, k):
        return pltpu.make_async_remote_copy(
            src_ref=src, dst_ref=before.at[k], send_sem=near_send.at[0, k], recv_sem=near_recv.at[0, k],
            device_id=place(lax.rem(me + 1, n)), device_id_type=MESH)

    def to_prev(src, k):
        return pltpu.make_async_remote_copy(
            src_ref=src, dst_ref=after.at[k], send_sem=near_send.at[1, k], recv_sem=near_recv.at[1, k],
            device_id=place(lax.rem(me + n - 1, n)), device_id_type=MESH)

    def share(src, k):
        @pl.when(me < n - 1)
        def _():
            to_next(src, k).start()

        @pl.when(me > 0)
        def _():
            to_prev(src, k).start()

    def receive(src, k):
        @pl.when(me > 0)
        def _():
            to_next(src, k).wait_recv()

        @pl.when(me < n - 1)
        def _():
            to_prev(src, k).wait_recv()

        @pl.when(me == 0)
        def _():
            before[k] = jnp.zeros((frames, neur_dev), F32)

        @pl.when(me == n - 1)
        def _():
            after[k] = jnp.zeros((frames, neur_dev), F32)

    def sent(src, k):
        @pl.when(me < n - 1)
        def _():
            to_next(src, k).wait_send()

        @pl.when(me > 0)
        def _():
            to_prev(src, k).wait_send()

    share(start, 0)

    def slot_copy(off):
        d = lax.rem(me + off, n)
        return pltpu.make_async_remote_copy(
            src_ref=slots.at[d], dst_ref=landed.at[me], send_sem=send_sem.at[d], recv_sem=recv_sem.at[me],
            device_id=place(d), device_id_type=MESH)

    @pl.loop(1, n)
    def _(off):
        slot_copy(off).start()

    eye = lax.broadcasted_iota(jnp.int32, (LANES, LANES), 0) == lax.broadcasted_iota(jnp.int32, (LANES, LANES), 1)
    for m in range(3):
        loads[m].wait()
        if m == 0:
            for b in range(0, neur_dev, LANES):
                block = raw[0, b:b + LANES, b:b + LANES]
                diag[:, b:b + LANES] = jnp.sum(jnp.where(eye, block, 0.0), axis=0, keepdims=True)
                raw[0, b:b + LANES, b:b + LANES] = jnp.where(eye, 0.0, block)

        @pl.loop(0, neur_dev // 16)
        def _(r):
            rows = pl.ds(pl.multiple_of(r * 16, 16), 16)
            hi, lo = halves(raw[m, rows, :])
            high[m, rows, :] = hi
            low[m, rows, :] = lo

    def product(c, m):
        hi, lo = halves(c)
        both = jnp.dot(jnp.concatenate([hi, lo], axis=0), high[m], preferred_element_type=F32)
        small = jnp.dot(hi, low[m], preferred_element_type=F32)
        return both[:frames] + (both[frames:] + small)

    receive(start, 0)
    coupled = product(start[...], 0) + product(before[0], 1) + product(after[0], 2)

    projected[...] = jnp.zeros_like(projected)
    number = lax.broadcasted_iota(jnp.int32, (neur_dev, LANES), 0).astype(F32)
    shift = (me * neur_dev).astype(F32)
    own.wait()

    @pl.loop(0, n // BATCH)
    def _(b):
        hots, values = [], []
        for s in range(BATCH):
            off = b * BATCH + s
            source = lax.rem(me + n - off, n)

            @pl.when(off > 0)
            def _():
                pltpu.make_async_remote_copy(
                    src_ref=slots.at[source], dst_ref=landed.at[source], send_sem=send_sem.at[source],
                    recv_sem=recv_sem.at[source], device_id=place(source), device_id_type=MESH).wait_recv()

        for s in range(BATCH):
            source = lax.rem(me + n - (b * BATCH + s), n)
            names = landed[source, frames:] - shift
            hots.append(jnp.where(number == names, 1.0, 0.0).astype(BF16))
            values.append(jnp.concatenate(halves(landed[source, :frames]), axis=0))
        projected[...] += lax.dot_general(
            jnp.concatenate(values, axis=1), jnp.concatenate(hots, axis=1), NT, preferred_element_type=F32)

    total = projected[:frames] + projected[frames:]
    scale = diag[...]
    for k in range(1, SWEEPS):
        current[k - 1] = jnp.maximum((total - coupled) / scale, 0.0)
        share(current.at[k - 1], k)
        coupled = product(current[k - 1], 0)
        receive(current.at[k - 1], k)
        coupled = coupled + product(before[k], 1) + product(after[k], 2)
    traces[...] = jnp.maximum((total - coupled) / scale, 0.0)

    sent(start, 0)
    for k in range(1, SWEEPS):
        sent(current.at[k - 1], k)

    @pl.loop(1, n)
    def _(off):
        slot_copy(off).wait_send()


def local(
    movie,
    entry_tile,
    entry_neuron,
    entry_weights,
    intersection_self,
    intersection_prev,
    intersection_next,
    prev_traces,
):
    n_rows = lax.axis_size("rows")
    n = lax.axis_size("planes") * n_rows
    frames, neur_dev = prev_traces.shape
    entries = entry_tile.shape[0]
    tiles = movie.shape[0]
    cap = 2 * entries // n
    whole = pl.BlockSpec(memory_space=pltpu.VMEM)
    scalar = pl.BlockSpec(memory_space=pltpu.SMEM)
    anywhere = pl.BlockSpec(memory_space=pl.ANY)
    slots = pl.pallas_call(
        functools.partial(contrib_kernel, cap, neur_dev),
        grid=(STEPS,),
        in_specs=[
            scalar,
            scalar,
            pl.BlockSpec((tiles // STEPS, frames * LANES), lambda i: (i, 0)),
            whole,
            whole,
        ],
        out_specs=pl.BlockSpec((n, frames + 1, LANES), lambda i: (0, 0, 0)),
        out_shape=jax.ShapeDtypeStruct((n, frames + 1, LANES), F32),
        scratch_shapes=[pltpu.VMEM((tiles * frames, LANES), F32)],
        compiler_params=pltpu.CompilerParams(vmem_limit_bytes=40 * 2**20),
        name="contrib",
    )(entry_tile, entry_neuron, movie, entry_weights, entry_neuron.reshape(entries // LANES, LANES))
    return pl.pallas_call(
        functools.partial(sweep_kernel, n, n_rows),
        in_specs=[anywhere] * 4 + [whole],
        out_specs=whole,
        out_shape=jax.ShapeDtypeStruct((frames, neur_dev), F32),
        scratch_shapes=[
            pltpu.VMEM((n, frames + 1, LANES), F32),
            pltpu.VMEM((3, neur_dev, neur_dev), F32),
            pltpu.VMEM((3, neur_dev, neur_dev), BF16),
            pltpu.VMEM((3, neur_dev, neur_dev), BF16),
            pltpu.VMEM((1, neur_dev), F32),
            pltpu.VMEM((2 * frames, neur_dev), F32),
            pltpu.VMEM((SWEEPS - 1, frames, neur_dev), F32),
            pltpu.VMEM((SWEEPS, frames, neur_dev), F32),
            pltpu.VMEM((SWEEPS, frames, neur_dev), F32),
            pltpu.SemaphoreType.DMA((3,)),
            pltpu.SemaphoreType.DMA,
            pltpu.SemaphoreType.DMA((n,)),
            pltpu.SemaphoreType.DMA((n,)),
            pltpu.SemaphoreType.DMA((2, SWEEPS)),
            pltpu.SemaphoreType.DMA((2, SWEEPS)),
        ],
        compiler_params=pltpu.CompilerParams(
            vmem_limit_bytes=40 * 2**20, collective_id=0, has_side_effects=True),
        name="sweeps",
    )(slots, intersection_self, intersection_prev, intersection_next, prev_traces)


def solution(mesh):
    spread = ("planes", "rows")
    return jax.shard_map(
        local,
        mesh=mesh,
        in_specs=(
            P(spread, None),
            P(spread),
            P(spread),
            P(spread, None),
            P(spread, None),
            P(spread, None),
            P(spread, None),
            P(None, spread),
        ),
        out_specs=P(None, spread),
        check_vma=False,
    )
```

```python
import functools

import jax
import jax.numpy as jnp
from jax import lax
from jax.experimental import pallas as pl
from jax.experimental.pallas import tpu as pltpu
from jax.sharding import PartitionSpec as P

SWEEPS = 3
LANES = 128
STEPS = 8
BATCH = 8
F32 = jnp.float32
BF16 = jnp.bfloat16
MESH = pl.DeviceIdType.MESH
NT = (((1,), (1,)), ((), ()))


def halves(x):
    hi = x.astype(BF16)
    return hi, (x - hi.astype(F32)).astype(BF16)


def trace_kernel(
    n,
    n_rows,
    cap,
    tile_h,
    neuron_h,
    names_h,
    movie_h,
    weights_h,
    self_h,
    prev_h,
    next_h,
    start_h,
    traces,
    tile_s,
    neuron_s,
    names_v,
    weights,
    start,
    movie,
    staged,
    contrib,
    slots,
    landed,
    raw,
    high,
    low,
    diag,
    projected,
    current,
    before,
    after,
    small_sem,
    movie_sem,
    raw_sem,
    send_sem,
    recv_sem,
    near_send,
    near_recv,
):
    me = lax.axis_index("planes") * n_rows + lax.axis_index("rows")
    frames, neur_dev = start.shape

    def place(d):
        return (d // n_rows, lax.rem(d, n_rows))

    small = [
        pltpu.make_async_copy(h, v, small_sem.at[i])
        for i, (h, v) in enumerate((
            (tile_h, tile_s), (neuron_h, neuron_s), (names_h, names_v), (weights_h, weights), (start_h, start)))
    ]
    tiles = movie.shape[0]
    rows = tiles // STEPS

    def piece(i):
        part = pl.ds(pl.multiple_of(i * rows, rows), rows)
        return pltpu.make_async_copy(movie_h.at[part], movie.at[part], movie_sem.at[i])

    for i in range(STEPS):
        piece(i).start()
    for copy in small:
        copy.start()
    loads = [pltpu.make_async_copy(h, raw.at[i], raw_sem.at[i]) for i, h in enumerate((self_h, prev_h, next_h))]
    for load in loads:
        load.start()

    barrier = pltpu.get_barrier_semaphore()

    @pl.loop(1, n)
    def _(off):
        pl.semaphore_signal(barrier, inc=1, device_id=place(lax.rem(me + off, n)), device_id_type=MESH)

    @pl.loop(0, STEPS)
    def _(i):
        piece(i).wait()

        @pl.loop(0, rows // 16)
        def _(r):
            base = pl.multiple_of(i * rows + r * 16, 16)
            for f in range(frames):
                x = movie[pl.ds(base, 16), f * LANES:(f + 1) * LANES].astype(F32)
                staged[pl.ds(base, 16), f, :] = x

    for copy in small:
        copy.wait()
    lane = lax.broadcasted_iota(jnp.int32, (frames, LANES), 1)
    part = 32

    @pl.loop(0, weights.shape[0] // LANES)
    def _(c):
        first = pl.multiple_of(c * LANES, LANES)
        w = weights[pl.ds(first, LANES), :]
        acc = jnp.zeros((frames, LANES), F32)
        for p in range(0, LANES, part):
            picked = [
                staged[tile_s[first + p + i]].astype(BF16)
                for i in range(part)
            ]
            prod = lax.dot_general(jnp.concatenate(picked, axis=0), w, NT, preferred_element_type=F32)
            for i in range(part):
                acc = jnp.where(lane == p + i, prod[i * frames:(i + 1) * frames], acc)
        contrib[c, :frames] = acc
        contrib[c, frames:] = names_v[pl.ds(c, 1), :].astype(F32)

    pl.semaphore_wait(barrier, n - 1)

    def to_next(src, k):
        return pltpu.make_async_remote_copy(
            src_ref=src, dst_ref=before.at[k], send_sem=near_send.at[0, k], recv_sem=near_recv.at[0, k],
            device_id=place(lax.rem(me + 1, n)), device_id_type=MESH)

    def to_prev(src, k):
        return pltpu.make_async_remote_copy(
            src_ref=src, dst_ref=after.at[k], send_sem=near_send.at[1, k], recv_sem=near_recv.at[1, k],
            device_id=place(lax.rem(me + n - 1, n)), device_id_type=MESH)

    def share(src, k):
        @pl.when(me < n - 1)
        def _():
            to_next(src, k).start()

        @pl.when(me > 0)
        def _():
            to_prev(src, k).start()

    def receive(src, k):
        @pl.when(me > 0)
        def _():
            to_next(src, k).wait_recv()

        @pl.when(me < n - 1)
        def _():
            to_prev(src, k).wait_recv()

        @pl.when(me == 0)
        def _():
            before[k] = jnp.zeros((frames, neur_dev), F32)

        @pl.when(me == n - 1)
        def _():
            after[k] = jnp.zeros((frames, neur_dev), F32)

    def sent(src, k):
        @pl.when(me < n - 1)
        def _():
            to_next(src, k).wait_send()

        @pl.when(me > 0)
        def _():
            to_prev(src, k).wait_send()

    share(start, 0)

    def group_of(d):
        low_end = d * neur_dev
        found = 0
        for head in range(0, tile_s.shape[0], cap):
            name = neuron_s[head]
            mine = jnp.logical_and(name >= low_end, name < low_end + neur_dev)
            found = jnp.where(mine, head // LANES, found)
        return found

    landed[me] = contrib[0]

    def slot_copy(off):
        d = lax.rem(me + off, n)
        return pltpu.make_async_remote_copy(
            src_ref=slots.at[d], dst_ref=landed.at[me], send_sem=send_sem.at[d], recv_sem=recv_sem.at[me],
            device_id=place(d), device_id_type=MESH)

    @pl.loop(1, n)
    def _(off):
        d = lax.rem(me + off, n)
        slots[d] = contrib[group_of(d)]
        slot_copy(off).start()

    eye = lax.broadcasted_iota(jnp.int32, (LANES, LANES), 0) == lax.broadcasted_iota(jnp.int32, (LANES, LANES), 1)
    for m in range(3):
        loads[m].wait()
        if m == 0:
            for b in range(0, neur_dev, LANES):
                block = raw[0, b:b + LANES, b:b + LANES]
                diag[:, b:b + LANES] = jnp.sum(jnp.where(eye, block, 0.0), axis=0, keepdims=True)
                raw[0, b:b + LANES, b:b + LANES] = jnp.where(eye, 0.0, block)

        @pl.loop(0, neur_dev // 16)
        def _(r):
            rows = pl.ds(pl.multiple_of(r * 16, 16), 16)
            hi, lo = halves(raw[m, rows, :])
            high[m, rows, :] = hi
            low[m, rows, :] = lo

    def product(c, m):
        hi, lo = halves(c)
        both = jnp.dot(jnp.concatenate([hi, lo], axis=0), high[m], preferred_element_type=F32)
        small = jnp.dot(hi, low[m], preferred_element_type=F32)
        return both[:frames] + (both[frames:] + small)

    receive(start, 0)
    coupled = product(start[...], 0) + product(before[0], 1) + product(after[0], 2)

    projected[...] = jnp.zeros_like(projected)
    number = lax.broadcasted_iota(jnp.int32, (neur_dev, LANES), 0).astype(F32)
    shift = (me * neur_dev).astype(F32)

    @pl.loop(0, n // BATCH)
    def _(b):
        hots, values = [], []
        for s in range(BATCH):
            off = b * BATCH + s
            source = lax.rem(me + n - off, n)

            @pl.when(off > 0)
            def _():
                pltpu.make_async_remote_copy(
                    src_ref=slots.at[source], dst_ref=landed.at[source], send_sem=send_sem.at[source],
                    recv_sem=recv_sem.at[source], device_id=place(source), device_id_type=MESH).wait_recv()

        for s in range(BATCH):
            source = lax.rem(me + n - (b * BATCH + s), n)
            names = landed[source, frames:] - shift
            hots.append(jnp.where(number == names, 1.0, 0.0).astype(BF16))
            values.append(jnp.concatenate(halves(landed[source, :frames]), axis=0))
        projected[...] += lax.dot_general(
            jnp.concatenate(values, axis=1), jnp.concatenate(hots, axis=1), NT, preferred_element_type=F32)

    total = projected[:frames] + projected[frames:]
    scale = diag[...]
    for k in range(1, SWEEPS):
        current[k - 1] = jnp.maximum((total - coupled) / scale, 0.0)
        share(current.at[k - 1], k)
        coupled = product(current[k - 1], 0)
        receive(current.at[k - 1], k)
        coupled = coupled + product(before[k], 1) + product(after[k], 2)
    traces[...] = jnp.maximum((total - coupled) / scale, 0.0)

    sent(start, 0)
    for k in range(1, SWEEPS):
        sent(current.at[k - 1], k)

    @pl.loop(1, n)
    def _(off):
        slot_copy(off).wait_send()


def local(
    movie,
    entry_tile,
    entry_neuron,
    entry_weights,
    intersection_self,
    intersection_prev,
    intersection_next,
    prev_traces,
):
    n_rows = lax.axis_size("rows")
    n = lax.axis_size("planes") * n_rows
    frames, neur_dev = prev_traces.shape
    entries = entry_tile.shape[0]
    tiles = movie.shape[0]
    cap = 2 * entries // n
    anywhere = pl.BlockSpec(memory_space=pl.ANY)
    chunks = entries // LANES
    voxels = entry_weights.shape[1]
    return pl.pallas_call(
        functools.partial(trace_kernel, n, n_rows, cap),
        in_specs=[anywhere] * 9,
        out_specs=pl.BlockSpec(memory_space=pltpu.VMEM),
        out_shape=jax.ShapeDtypeStruct((frames, neur_dev), F32),
        scratch_shapes=[
            pltpu.SMEM((entries,), jnp.int32),
            pltpu.SMEM((entries,), jnp.int32),
            pltpu.VMEM((chunks, LANES), jnp.int32),
            pltpu.VMEM((entries, voxels), BF16),
            pltpu.VMEM((frames, neur_dev), F32),
            pltpu.VMEM((tiles, frames * voxels), BF16),
            pltpu.VMEM((tiles, frames, LANES), F32),
            pltpu.VMEM((chunks, frames + 1, LANES), F32),
            pltpu.VMEM((n, frames + 1, LANES), F32),
            pltpu.VMEM((n, frames + 1, LANES), F32),
            pltpu.VMEM((3, neur_dev, neur_dev), F32),
            pltpu.VMEM((3, neur_dev, neur_dev), BF16),
            pltpu.VMEM((3, neur_dev, neur_dev), BF16),
            pltpu.VMEM((1, neur_dev), F32),
            pltpu.VMEM((2 * frames, neur_dev), F32),
            pltpu.VMEM((SWEEPS - 1, frames, neur_dev), F32),
            pltpu.VMEM((SWEEPS, frames, neur_dev), F32),
            pltpu.VMEM((SWEEPS, frames, neur_dev), F32),
            pltpu.SemaphoreType.DMA((5,)),
            pltpu.SemaphoreType.DMA((STEPS,)),
            pltpu.SemaphoreType.DMA((3,)),
            pltpu.SemaphoreType.DMA((n,)),
            pltpu.SemaphoreType.DMA((n,)),
            pltpu.SemaphoreType.DMA((2, SWEEPS)),
            pltpu.SemaphoreType.DMA((2, SWEEPS)),
        ],
        compiler_params=pltpu.CompilerParams(
            vmem_limit_bytes=60 * 2**20, collective_id=0, has_side_effects=True),
        name="traces",
    )(
        entry_tile,
        entry_neuron,
        entry_neuron.reshape(chunks, LANES),
        movie,
        entry_weights,
        intersection_self,
        intersection_prev,
        intersection_next,
        prev_traces,
    )


def solution(mesh):
    spread = ("planes", "rows")
    return jax.shard_map(
        local,
        mesh=mesh,
        in_specs=(
            P(spread, None),
            P(spread),
            P(spread),
            P(spread, None),
            P(spread, None),
            P(spread, None),
            P(spread, None),
            P(None, spread),
        ),
        out_specs=P(None, spread),
        check_vma=False,
    )
```

```python
import functools

import jax
import jax.numpy as jnp
from jax import lax
from jax.experimental import pallas as pl
from jax.experimental.pallas import tpu as pltpu
from jax.sharding import PartitionSpec as P

SWEEPS = 3
LANES = 128
STEPS = 8
BATCH = 8
F32 = jnp.float32
BF16 = jnp.bfloat16
MESH = pl.DeviceIdType.MESH
NT = (((1,), (1,)), ((), ()))


def halves(x):
    hi = x.astype(BF16)
    return hi, (x - hi.astype(F32)).astype(BF16)


def trace_kernel(
    n,
    n_rows,
    cap,
    tile_h,
    neuron_h,
    names_h,
    movie_h,
    weights_h,
    self_h,
    prev_h,
    next_h,
    start_h,
    traces,
    tile_s,
    neuron_s,
    names_v,
    weights,
    start,
    movie,
    staged,
    contrib,
    slots,
    landed,
    raw,
    high,
    low,
    diag,
    projected,
    current,
    before,
    after,
    small_sem,
    movie_sem,
    raw_sem,
    send_sem,
    recv_sem,
    near_send,
    near_recv,
):
    me = lax.axis_index("planes") * n_rows + lax.axis_index("rows")
    frames, neur_dev = start.shape

    def place(d):
        return (d // n_rows, lax.rem(d, n_rows))

    small = [
        pltpu.make_async_copy(h, v, small_sem.at[i])
        for i, (h, v) in enumerate((
            (tile_h, tile_s), (neuron_h, neuron_s), (names_h, names_v), (weights_h, weights), (start_h, start)))
    ]
    tiles = movie.shape[0]
    rows = tiles // STEPS

    def piece(i):
        part = pl.ds(pl.multiple_of(i * rows, rows), rows)
        return pltpu.make_async_copy(movie_h.at[part], movie.at[part], movie_sem.at[i])

    for i in range(STEPS):
        piece(i).start()
    for copy in small:
        copy.start()
    loads = [pltpu.make_async_copy(h, raw.at[i], raw_sem.at[i]) for i, h in enumerate((self_h, prev_h, next_h))]
    for load in loads:
        load.start()

    barrier = pltpu.get_barrier_semaphore()

    @pl.loop(1, n)
    def _(off):
        pl.semaphore_signal(barrier, inc=1, device_id=place(lax.rem(me + off, n)), device_id_type=MESH)

    flat = staged.reshape(tiles * frames, LANES)

    @pl.loop(0, STEPS)
    def _(i):
        piece(i).wait()

        @pl.loop(0, rows // 16)
        def _(r):
            base = pl.multiple_of(i * rows + r * 16, 16)
            for f in range(frames):
                x = movie[pl.ds(base, 16), f * LANES:(f + 1) * LANES].astype(F32)
                flat[pl.ds(base * frames + f, 16, stride=frames), :] = x

    for copy in small:
        copy.wait()
    lane = lax.broadcasted_iota(jnp.int32, (frames, LANES), 1)
    part = 32

    @pl.loop(0, weights.shape[0] // (2 * LANES))
    def _(pair):
        for half in range(2):
            c = pair * 2 + half
            first = pl.multiple_of(c * LANES, LANES)
            w = weights[pl.ds(first, LANES), :].astype(F32).T.astype(BF16)
            acc = jnp.zeros((frames, LANES), F32)
            for p in range(0, LANES, part):
                picked = [staged[tile_s[first + p + i]].astype(BF16) for i in range(part)]
                prod = jnp.dot(jnp.concatenate(picked, axis=0), w, preferred_element_type=F32)
                for i in range(part):
                    acc = jnp.where(lane == p + i, prod[i * frames:(i + 1) * frames], acc)
            contrib[c, :frames] = acc
            contrib[c, frames:] = names_v[pl.ds(c, 1), :].astype(F32)

    def group_of(d):
        low_end = d * neur_dev
        found = 0
        for head in range(0, tile_s.shape[0], cap):
            name = neuron_s[head]
            mine = jnp.logical_and(name >= low_end, name < low_end + neur_dev)
            found = jnp.where(mine, head // LANES, found)
        return found

    landed[me] = contrib[0]

    @pl.loop(1, n)
    def _(off):
        d = lax.rem(me + off, n)
        slots[d] = contrib[group_of(d)]

    pl.semaphore_wait(barrier, n - 1)

    def to_next(src, k):
        return pltpu.make_async_remote_copy(
            src_ref=src, dst_ref=before.at[k], send_sem=near_send.at[0, k], recv_sem=near_recv.at[0, k],
            device_id=place(lax.rem(me + 1, n)), device_id_type=MESH)

    def to_prev(src, k):
        return pltpu.make_async_remote_copy(
            src_ref=src, dst_ref=after.at[k], send_sem=near_send.at[1, k], recv_sem=near_recv.at[1, k],
            device_id=place(lax.rem(me + n - 1, n)), device_id_type=MESH)

    def share(src, k):
        @pl.when(me < n - 1)
        def _():
            to_next(src, k).start()

        @pl.when(me > 0)
        def _():
            to_prev(src, k).start()

    def receive(src, k):
        @pl.when(me > 0)
        def _():
            to_next(src, k).wait_recv()

        @pl.when(me < n - 1)
        def _():
            to_prev(src, k).wait_recv()

        @pl.when(me == 0)
        def _():
            before[k] = jnp.zeros((frames, neur_dev), F32)

        @pl.when(me == n - 1)
        def _():
            after[k] = jnp.zeros((frames, neur_dev), F32)

    def sent(src, k):
        @pl.when(me < n - 1)
        def _():
            to_next(src, k).wait_send()

        @pl.when(me > 0)
        def _():
            to_prev(src, k).wait_send()

    share(start, 0)

    def slot_copy(off):
        d = lax.rem(me + off, n)
        return pltpu.make_async_remote_copy(
            src_ref=slots.at[d], dst_ref=landed.at[me], send_sem=send_sem.at[d], recv_sem=recv_sem.at[me],
            device_id=place(d), device_id_type=MESH)

    @pl.loop(1, n)
    def _(off):
        slot_copy(off).start()

    eye = lax.broadcasted_iota(jnp.int32, (LANES, LANES), 0) == lax.broadcasted_iota(jnp.int32, (LANES, LANES), 1)
    for m in range(3):
        loads[m].wait()
        if m == 0:
            for b in range(0, neur_dev, LANES):
                block = raw[0, b:b + LANES, b:b + LANES]
                diag[:, b:b + LANES] = jnp.sum(jnp.where(eye, block, 0.0), axis=0, keepdims=True)
                raw[0, b:b + LANES, b:b + LANES] = jnp.where(eye, 0.0, block)

        @pl.loop(0, neur_dev // 16)
        def _(r):
            rows = pl.ds(pl.multiple_of(r * 16, 16), 16)
            hi, lo = halves(raw[m, rows, :])
            high[m, rows, :] = hi
            low[m, rows, :] = lo

    def product(c, m):
        hi, lo = halves(c)
        both = jnp.dot(jnp.concatenate([hi, lo], axis=0), high[m], preferred_element_type=F32)
        small = jnp.dot(hi, low[m], preferred_element_type=F32)
        return both[:frames] + (both[frames:] + small)

    receive(start, 0)
    coupled = product(start[...], 0) + product(before[0], 1) + product(after[0], 2)

    projected[...] = jnp.zeros_like(projected)
    number = lax.broadcasted_iota(jnp.int32, (neur_dev, LANES), 0).astype(F32)
    shift = (me * neur_dev).astype(F32)

    @pl.loop(0, n // BATCH)
    def _(b):
        hots, values = [], []
        for s in range(BATCH):
            off = b * BATCH + s
            source = lax.rem(me + n - off, n)

            @pl.when(off > 0)
            def _():
                pltpu.make_async_remote_copy(
                    src_ref=slots.at[source], dst_ref=landed.at[source], send_sem=send_sem.at[source],
                    recv_sem=recv_sem.at[source], device_id=place(source), device_id_type=MESH).wait_recv()

        for s in range(BATCH):
            source = lax.rem(me + n - (b * BATCH + s), n)
            names = landed[source, frames:] - shift
            hots.append(jnp.where(number == names, 1.0, 0.0).astype(BF16))
            values.append(jnp.concatenate(halves(landed[source, :frames]), axis=0))
        projected[:, :2 * frames] += lax.dot_general(
            jnp.concatenate(hots, axis=1), jnp.concatenate(values, axis=1), NT, preferred_element_type=F32)

    sums = projected[...].T
    total = sums[:frames] + sums[frames:2 * frames]
    scale = diag[...]
    for k in range(1, SWEEPS):
        current[k - 1] = jnp.maximum((total - coupled) / scale, 0.0)
        share(current.at[k - 1], k)
        coupled = product(current[k - 1], 0)
        receive(current.at[k - 1], k)
        coupled = coupled + product(before[k], 1) + product(after[k], 2)
    traces[...] = jnp.maximum((total - coupled) / scale, 0.0)

    sent(start, 0)
    for k in range(1, SWEEPS):
        sent(current.at[k - 1], k)

    @pl.loop(1, n)
    def _(off):
        slot_copy(off).wait_send()


def local(
    movie,
    entry_tile,
    entry_neuron,
    entry_weights,
    intersection_self,
    intersection_prev,
    intersection_next,
    prev_traces,
):
    n_rows = lax.axis_size("rows")
    n = lax.axis_size("planes") * n_rows
    frames, neur_dev = prev_traces.shape
    entries = entry_tile.shape[0]
    tiles = movie.shape[0]
    cap = 2 * entries // n
    anywhere = pl.BlockSpec(memory_space=pl.ANY)
    chunks = entries // LANES
    voxels = entry_weights.shape[1]
    return pl.pallas_call(
        functools.partial(trace_kernel, n, n_rows, cap),
        in_specs=[anywhere] * 9,
        out_specs=pl.BlockSpec(memory_space=pltpu.VMEM),
        out_shape=jax.ShapeDtypeStruct((frames, neur_dev), F32),
        scratch_shapes=[
            pltpu.SMEM((entries,), jnp.int32),
            pltpu.SMEM((entries,), jnp.int32),
            pltpu.VMEM((chunks, LANES), jnp.int32),
            pltpu.VMEM((entries, voxels), BF16),
            pltpu.VMEM((frames, neur_dev), F32),
            pltpu.VMEM((tiles, frames * voxels), BF16),
            pltpu.VMEM((tiles, frames, LANES), F32),
            pltpu.VMEM((chunks, frames + 1, LANES), F32),
            pltpu.VMEM((n, frames + 1, LANES), F32),
            pltpu.VMEM((n, frames + 1, LANES), F32),
            pltpu.VMEM((3, neur_dev, neur_dev), F32),
            pltpu.VMEM((3, neur_dev, neur_dev), BF16),
            pltpu.VMEM((3, neur_dev, neur_dev), BF16),
            pltpu.VMEM((1, neur_dev), F32),
            pltpu.VMEM((neur_dev, LANES), F32),
            pltpu.VMEM((SWEEPS - 1, frames, neur_dev), F32),
            pltpu.VMEM((SWEEPS, frames, neur_dev), F32),
            pltpu.VMEM((SWEEPS, frames, neur_dev), F32),
            pltpu.SemaphoreType.DMA((5,)),
            pltpu.SemaphoreType.DMA((STEPS,)),
            pltpu.SemaphoreType.DMA((3,)),
            pltpu.SemaphoreType.DMA((n,)),
            pltpu.SemaphoreType.DMA((n,)),
            pltpu.SemaphoreType.DMA((2, SWEEPS)),
            pltpu.SemaphoreType.DMA((2, SWEEPS)),
        ],
        compiler_params=pltpu.CompilerParams(
            vmem_limit_bytes=60 * 2**20, collective_id=0, has_side_effects=True),
        name="traces",
    )(
        entry_tile,
        entry_neuron,
        entry_neuron.reshape(chunks, LANES),
        movie,
        entry_weights,
        intersection_self,
        intersection_prev,
        intersection_next,
        prev_traces,
    )


def solution(mesh):
    spread = ("planes", "rows")
    return jax.shard_map(
        local,
        mesh=mesh,
        in_specs=(
            P(spread, None),
            P(spread),
            P(spread),
            P(spread, None),
            P(spread, None),
            P(spread, None),
            P(spread, None),
            P(None, spread),
        ),
        out_specs=P(None, spread),
        check_vma=False,
    )
```

```python
import functools

import jax
import jax.numpy as jnp
from jax import lax
from jax.experimental import pallas as pl
from jax.experimental.pallas import tpu as pltpu
from jax.sharding import PartitionSpec as P

SWEEPS = 3
LANES = 128
STEPS = 8
BATCH = 8
ZONE = 8
F32 = jnp.float32
BF16 = jnp.bfloat16
MESH = pl.DeviceIdType.MESH
NT = (((1,), (1,)), ((), ()))


def halves(x):
    hi = x.astype(BF16)
    return hi, (x - hi.astype(F32)).astype(BF16)


def trace_kernel(
    n,
    n_rows,
    cap,
    tile_h,
    neuron_h,
    names_h,
    movie_h,
    weights_h,
    self_h,
    prev_h,
    next_h,
    start_h,
    traces,
    tile_s,
    neuron_s,
    chunk_of,
    names_v,
    weights,
    start,
    movie,
    staged,
    contrib,
    slots,
    landed,
    raw,
    high,
    low,
    diag,
    projected,
    current,
    before,
    after,
    small_sem,
    movie_sem,
    raw_sem,
    send_sem,
    recv_sem,
    near_send,
    near_recv,
):
    me = lax.axis_index("planes") * n_rows + lax.axis_index("rows")
    frames, neur_dev = start.shape

    def place(d):
        return (d // n_rows, lax.rem(d, n_rows))

    small = [
        pltpu.make_async_copy(h, v, small_sem.at[i])
        for i, (h, v) in enumerate((
            (tile_h, tile_s), (neuron_h, neuron_s), (names_h, names_v), (weights_h, weights), (start_h, start)))
    ]
    tiles = movie.shape[0]
    rows = tiles // STEPS

    def piece(i):
        part = pl.ds(pl.multiple_of(i * rows, rows), rows)
        return pltpu.make_async_copy(movie_h.at[part], movie.at[part], movie_sem.at[i])

    for i in range(STEPS):
        piece(i).start()
    for copy in small:
        copy.start()
    zones = n // ZONE
    zone, member = lax.div(me, ZONE), lax.rem(me, ZONE)

    def turn(k):
        return lax.rem(lax.div(k, ZONE) + 1, zones), lax.rem(lax.rem(k, ZONE) + 1, ZONE)

    def target(k):
        a, b = turn(k)
        return lax.rem(zone + a, zones) * ZONE + lax.rem(member + b, ZONE)

    def origin(k):
        a, b = turn(k)
        return lax.rem(zone + zones - a, zones) * ZONE + lax.rem(member + ZONE - b, ZONE)

    loads = [pltpu.make_async_copy(h, raw.at[i], raw_sem.at[i]) for i, h in enumerate((self_h, prev_h, next_h))]
    for load in loads:
        load.start()

    barrier = pltpu.get_barrier_semaphore()

    @pl.loop(1, n)
    def _(off):
        pl.semaphore_signal(barrier, inc=1, device_id=place(lax.rem(me + off, n)), device_id_type=MESH)

    flat = staged.reshape(tiles * frames, LANES)

    @pl.loop(0, STEPS)
    def _(i):
        piece(i).wait()

        @pl.loop(0, rows // 16)
        def _(r):
            base = pl.multiple_of(i * rows + r * 16, 16)
            for f in range(frames):
                x = movie[pl.ds(base, 16), f * LANES:(f + 1) * LANES].astype(F32)
                flat[pl.ds(base * frames + f, 16, stride=frames), :] = x

    for copy in small:
        copy.wait()
    lane = lax.broadcasted_iota(jnp.int32, (frames, LANES), 1)
    part = 32

    def group_of(d):
        low_end = d * neur_dev
        found = 0
        for head in range(0, tile_s.shape[0], cap):
            name = neuron_s[head]
            mine = jnp.logical_and(name >= low_end, name < low_end + neur_dev)
            found = jnp.where(mine, head // LANES, found)
        return found

    pairs = weights.shape[0] // (2 * LANES)

    @pl.loop(0, pairs)
    def _(pair):
        for j in range(n // pairs):
            d = pair * (n // pairs) + j
            chunk_of[d] = group_of(d)
        for half in range(2):
            c = pair * 2 + half
            first = pl.multiple_of(c * LANES, LANES)
            w = weights[pl.ds(first, LANES), :].astype(F32).T.astype(BF16)
            acc = jnp.zeros((frames, LANES), F32)
            for p in range(0, LANES, part):
                picked = [staged[tile_s[first + p + i]].astype(BF16) for i in range(part)]
                prod = jnp.dot(jnp.concatenate(picked, axis=0), w, preferred_element_type=F32)
                for i in range(part):
                    acc = jnp.where(lane == p + i, prod[i * frames:(i + 1) * frames], acc)
            contrib[c, :frames] = acc
            contrib[c, frames:] = names_v[pl.ds(c, 1), :].astype(F32)

    for d in range(n):
        slots[d] = contrib[chunk_of[d]]
    landed[me] = contrib[0]

    pl.semaphore_wait(barrier, n - 1)

    def to_next(src, k):
        return pltpu.make_async_remote_copy(
            src_ref=src, dst_ref=before.at[k], send_sem=near_send.at[0, k], recv_sem=near_recv.at[0, k],
            device_id=place(lax.rem(me + 1, n)), device_id_type=MESH)

    def to_prev(src, k):
        return pltpu.make_async_remote_copy(
            src_ref=src, dst_ref=after.at[k], send_sem=near_send.at[1, k], recv_sem=near_recv.at[1, k],
            device_id=place(lax.rem(me + n - 1, n)), device_id_type=MESH)

    def share(src, k):
        @pl.when(me < n - 1)
        def _():
            to_next(src, k).start()

        @pl.when(me > 0)
        def _():
            to_prev(src, k).start()

    def receive_before(src, k):
        @pl.when(me > 0)
        def _():
            to_next(src, k).wait_recv()

        @pl.when(me == 0)
        def _():
            before[k] = jnp.zeros((frames, neur_dev), F32)

    def receive_after(src, k):
        @pl.when(me < n - 1)
        def _():
            to_prev(src, k).wait_recv()

        @pl.when(me == n - 1)
        def _():
            after[k] = jnp.zeros((frames, neur_dev), F32)

    def sent(src, k):
        @pl.when(me < n - 1)
        def _():
            to_next(src, k).wait_send()

        @pl.when(me > 0)
        def _():
            to_prev(src, k).wait_send()

    share(start, 0)

    def slot_copy(k):
        d = target(k)
        return pltpu.make_async_remote_copy(
            src_ref=slots.at[d], dst_ref=landed.at[me], send_sem=send_sem.at[d], recv_sem=recv_sem.at[me],
            device_id=place(d), device_id_type=MESH)

    @pl.loop(0, n - 1)
    def _(k):
        slot_copy(k).start()

    eye = lax.broadcasted_iota(jnp.int32, (LANES, LANES), 0) == lax.broadcasted_iota(jnp.int32, (LANES, LANES), 1)
    for m in range(3):
        loads[m].wait()
        if m == 0:
            for b in range(0, neur_dev, LANES):
                block = raw[0, b:b + LANES, b:b + LANES]
                diag[:, b:b + LANES] = jnp.sum(jnp.where(eye, block, 0.0), axis=0, keepdims=True)
                raw[0, b:b + LANES, b:b + LANES] = jnp.where(eye, 0.0, block)

        @pl.loop(0, neur_dev // 16)
        def _(r):
            rows = pl.ds(pl.multiple_of(r * 16, 16), 16)
            hi, lo = halves(raw[m, rows, :])
            high[m, rows, :] = hi
            low[m, rows, :] = lo

    def product(c, m):
        hi, lo = halves(c)
        both = jnp.dot(jnp.concatenate([hi, lo], axis=0), high[m], preferred_element_type=F32)
        small = jnp.dot(hi, low[m], preferred_element_type=F32)
        return both[:frames] + (both[frames:] + small)

    receive_before(start, 0)
    receive_after(start, 0)
    coupled = product(start[...], 0) + product(before[0], 1) + product(after[0], 2)

    projected[...] = jnp.zeros_like(projected)
    number = lax.broadcasted_iota(jnp.int32, (neur_dev, LANES), 0).astype(F32)
    shift = (me * neur_dev).astype(F32)

    @pl.loop(0, n // BATCH)
    def _(b):
        hots, values = [], []
        for s in range(BATCH):
            k = b * BATCH + s
            source = origin(k)

            @pl.when(k < n - 1)
            def _():
                pltpu.make_async_remote_copy(
                    src_ref=slots.at[source], dst_ref=landed.at[source], send_sem=send_sem.at[source],
                    recv_sem=recv_sem.at[source], device_id=place(source), device_id_type=MESH).wait_recv()

        for s in range(BATCH):
            source = origin(b * BATCH + s)
            names = landed[source, frames:] - shift
            hots.append(jnp.where(number == names, 1.0, 0.0).astype(BF16))
            values.append(jnp.concatenate(halves(landed[source, :frames]), axis=0))
        projected[:, :2 * frames] += lax.dot_general(
            jnp.concatenate(hots, axis=1), jnp.concatenate(values, axis=1), NT, preferred_element_type=F32)

    sums = projected[...].T
    total = sums[:frames] + sums[frames:2 * frames]
    scale = diag[...]
    for k in range(1, SWEEPS):
        current[k - 1] = jnp.maximum((total - coupled) / scale, 0.0)
        share(current.at[k - 1], k)
        coupled = product(current[k - 1], 0)
        receive_before(current.at[k - 1], k)
        coupled = coupled + product(before[k], 1)
        receive_after(current.at[k - 1], k)
        coupled = coupled + product(after[k], 2)
    traces[...] = jnp.maximum((total - coupled) / scale, 0.0)

    sent(start, 0)
    for k in range(1, SWEEPS):
        sent(current.at[k - 1], k)

    @pl.loop(0, n - 1)
    def _(k):
        slot_copy(k).wait_send()


def local(
    movie,
    entry_tile,
    entry_neuron,
    entry_weights,
    intersection_self,
    intersection_prev,
    intersection_next,
    prev_traces,
):
    n_rows = lax.axis_size("rows")
    n = lax.axis_size("planes") * n_rows
    frames, neur_dev = prev_traces.shape
    entries = entry_tile.shape[0]
    tiles = movie.shape[0]
    cap = 2 * entries // n
    anywhere = pl.BlockSpec(memory_space=pl.ANY)
    chunks = entries // LANES
    voxels = entry_weights.shape[1]
    return pl.pallas_call(
        functools.partial(trace_kernel, n, n_rows, cap),
        in_specs=[anywhere] * 9,
        out_specs=pl.BlockSpec(memory_space=pltpu.VMEM),
        out_shape=jax.ShapeDtypeStruct((frames, neur_dev), F32),
        scratch_shapes=[
            pltpu.SMEM((entries,), jnp.int32),
            pltpu.SMEM((entries,), jnp.int32),
            pltpu.SMEM((n,), jnp.int32),
            pltpu.VMEM((chunks, LANES), jnp.int32),
            pltpu.VMEM((entries, voxels), BF16),
            pltpu.VMEM((frames, neur_dev), F32),
            pltpu.VMEM((tiles, frames * voxels), BF16),
            pltpu.VMEM((tiles, frames, LANES), F32),
            pltpu.VMEM((chunks, frames + 1, LANES), F32),
            pltpu.VMEM((n, frames + 1, LANES), F32),
            pltpu.VMEM((n, frames + 1, LANES), F32),
            pltpu.VMEM((3, neur_dev, neur_dev), F32),
            pltpu.VMEM((3, neur_dev, neur_dev), BF16),
            pltpu.VMEM((3, neur_dev, neur_dev), BF16),
            pltpu.VMEM((1, neur_dev), F32),
            pltpu.VMEM((neur_dev, LANES), F32),
            pltpu.VMEM((SWEEPS - 1, frames, neur_dev), F32),
            pltpu.VMEM((SWEEPS, frames, neur_dev), F32),
            pltpu.VMEM((SWEEPS, frames, neur_dev), F32),
            pltpu.SemaphoreType.DMA((5,)),
            pltpu.SemaphoreType.DMA((STEPS,)),
            pltpu.SemaphoreType.DMA((3,)),
            pltpu.SemaphoreType.DMA((n,)),
            pltpu.SemaphoreType.DMA((n,)),
            pltpu.SemaphoreType.DMA((2, SWEEPS)),
            pltpu.SemaphoreType.DMA((2, SWEEPS)),
        ],
        compiler_params=pltpu.CompilerParams(
            vmem_limit_bytes=60 * 2**20, collective_id=0, has_side_effects=True),
        name="traces",
    )(
        entry_tile,
        entry_neuron,
        entry_neuron.reshape(chunks, LANES),
        movie,
        entry_weights,
        intersection_self,
        intersection_prev,
        intersection_next,
        prev_traces,
    )


def solution(mesh):
    spread = ("planes", "rows")
    return jax.shard_map(
        local,
        mesh=mesh,
        in_specs=(
            P(spread, None),
            P(spread),
            P(spread),
            P(spread, None),
            P(spread, None),
            P(spread, None),
            P(spread, None),
            P(None, spread),
        ),
        out_specs=P(None, spread),
        check_vma=False,
    )
```

```python
import functools

import jax
import jax.numpy as jnp
from jax import lax
from jax.experimental import pallas as pl
from jax.experimental.pallas import tpu as pltpu
from jax.sharding import PartitionSpec as P

SWEEPS = 3
LANES = 128
STEPS = 8
BATCH = 8
ZONE = 8
F32 = jnp.float32
BF16 = jnp.bfloat16
MESH = pl.DeviceIdType.MESH
NT = (((1,), (1,)), ((), ()))


def halves(x):
    hi = x.astype(BF16)
    return hi, (x - hi.astype(F32)).astype(BF16)


def trace_kernel(
    n,
    n_rows,
    cap,
    tile_h,
    neuron_h,
    names_h,
    movie_h,
    weights_h,
    self_h,
    prev_h,
    next_h,
    start_h,
    traces,
    tile_s,
    neuron_s,
    chunk_of,
    names_v,
    weights,
    start,
    movie,
    staged,
    contrib,
    slots,
    landed,
    raw,
    high,
    low,
    diag,
    projected,
    current,
    before,
    after,
    small_sem,
    movie_sem,
    raw_sem,
    send_sem,
    recv_sem,
    near_send,
    near_recv,
):
    me = lax.axis_index("planes") * n_rows + lax.axis_index("rows")
    frames, neur_dev = start.shape

    def place(d):
        return (d // n_rows, lax.rem(d, n_rows))

    small = [
        pltpu.make_async_copy(h, v, small_sem.at[i])
        for i, (h, v) in enumerate((
            (tile_h, tile_s), (neuron_h, neuron_s), (names_h, names_v), (weights_h, weights), (start_h, start)))
    ]
    tiles = movie.shape[0]
    rows = tiles // STEPS

    def piece(i):
        part = pl.ds(pl.multiple_of(i * rows, rows), rows)
        return pltpu.make_async_copy(movie_h.at[part], movie.at[part], movie_sem.at[i])

    for i in range(STEPS):
        piece(i).start()
    for copy in small:
        copy.start()
    zones = n // ZONE
    zone, member = lax.div(me, ZONE), lax.rem(me, ZONE)

    def turn(k):
        return lax.rem(lax.div(k, ZONE) + 1, zones), lax.rem(lax.rem(k, ZONE) + 1, ZONE)

    def target(k):
        a, b = turn(k)
        return lax.rem(zone + a, zones) * ZONE + lax.rem(member + b, ZONE)

    def origin(k):
        a, b = turn(k)
        return lax.rem(zone + zones - a, zones) * ZONE + lax.rem(member + ZONE - b, ZONE)

    loads = [pltpu.make_async_copy(h, raw.at[i], raw_sem.at[i]) for i, h in enumerate((self_h, prev_h, next_h))]
    for load in loads:
        load.start()

    barrier = pltpu.get_barrier_semaphore()

    @pl.loop(1, n)
    def _(off):
        pl.semaphore_signal(barrier, inc=1, device_id=place(lax.rem(me + off, n)), device_id_type=MESH)

    flat = staged.reshape(tiles * frames, LANES)

    @pl.loop(0, STEPS)
    def _(i):
        piece(i).wait()

        @pl.loop(0, rows // 64)
        def _(r):
            for q in range(0, 64, 16):
                base = pl.multiple_of(i * rows + r * 64 + q, 16)
                for f in range(frames):
                    x = movie[pl.ds(base, 16), f * LANES:(f + 1) * LANES].astype(F32)
                    flat[pl.ds(base * frames + f, 16, stride=frames), :] = x

    for copy in small:
        copy.wait()
    lane = lax.broadcasted_iota(jnp.int32, (frames, LANES), 1)
    part = 32

    def group_of(d):
        low_end = d * neur_dev
        found = 0
        for head in range(0, tile_s.shape[0], cap):
            name = neuron_s[head]
            mine = jnp.logical_and(name >= low_end, name < low_end + neur_dev)
            found = jnp.where(mine, head // LANES, found)
        return found

    pairs = weights.shape[0] // (2 * LANES)

    @pl.loop(0, pairs)
    def _(pair):
        for j in range(n // pairs):
            d = pair * (n // pairs) + j
            chunk_of[d] = group_of(d)
        for half in range(2):
            c = pair * 2 + half
            first = pl.multiple_of(c * LANES, LANES)
            w = weights[pl.ds(first, LANES), :].astype(F32).T.astype(BF16)
            acc = jnp.zeros((frames, LANES), F32)
            for p in range(0, LANES, part):
                picked = [staged[tile_s[first + p + i]].astype(BF16) for i in range(part)]
                prod = jnp.dot(jnp.concatenate(picked, axis=0), w, preferred_element_type=F32)
                for i in range(part):
                    acc = jnp.where(lane == p + i, prod[i * frames:(i + 1) * frames], acc)
            contrib[c, :frames] = acc
            contrib[c, frames:] = names_v[pl.ds(c, 1), :].astype(F32)

    for d in range(n):
        slots[d] = contrib[chunk_of[d]]
    landed[me] = contrib[0]

    pl.semaphore_wait(barrier, n - 1)

    def to_next(src, k):
        return pltpu.make_async_remote_copy(
            src_ref=src, dst_ref=before.at[k], send_sem=near_send.at[0, k], recv_sem=near_recv.at[0, k],
            device_id=place(lax.rem(me + 1, n)), device_id_type=MESH)

    def to_prev(src, k):
        return pltpu.make_async_remote_copy(
            src_ref=src, dst_ref=after.at[k], send_sem=near_send.at[1, k], recv_sem=near_recv.at[1, k],
            device_id=place(lax.rem(me + n - 1, n)), device_id_type=MESH)

    def share(src, k):
        @pl.when(me < n - 1)
        def _():
            to_next(src, k).start()

        @pl.when(me > 0)
        def _():
            to_prev(src, k).start()

    def receive_before(src, k):
        @pl.when(me > 0)
        def _():
            to_next(src, k).wait_recv()

        @pl.when(me == 0)
        def _():
            before[k] = jnp.zeros((frames, neur_dev), F32)

    def receive_after(src, k):
        @pl.when(me < n - 1)
        def _():
            to_prev(src, k).wait_recv()

        @pl.when(me == n - 1)
        def _():
            after[k] = jnp.zeros((frames, neur_dev), F32)

    def sent(src, k):
        @pl.when(me < n - 1)
        def _():
            to_next(src, k).wait_send()

        @pl.when(me > 0)
        def _():
            to_prev(src, k).wait_send()

    share(start, 0)

    def slot_copy(k):
        d = target(k)
        return pltpu.make_async_remote_copy(
            src_ref=slots.at[d], dst_ref=landed.at[me], send_sem=send_sem.at[d], recv_sem=recv_sem.at[me],
            device_id=place(d), device_id_type=MESH)

    @pl.loop(0, n - 1)
    def _(k):
        slot_copy(k).start()

    eye = lax.broadcasted_iota(jnp.int32, (LANES, LANES), 0) == lax.broadcasted_iota(jnp.int32, (LANES, LANES), 1)
    for m in range(3):
        loads[m].wait()
        if m == 0:
            for b in range(0, neur_dev, LANES):
                block = raw[0, b:b + LANES, b:b + LANES]
                diag[:, b:b + LANES] = jnp.sum(jnp.where(eye, block, 0.0), axis=0, keepdims=True)
                raw[0, b:b + LANES, b:b + LANES] = jnp.where(eye, 0.0, block)

        @pl.loop(0, neur_dev // 64)
        def _(r):
            rows = pl.ds(pl.multiple_of(r * 64, 64), 64)
            hi, lo = halves(raw[m, rows, :])
            high[m, rows, :] = hi
            low[m, rows, :] = lo

    def product(c, m):
        hi, lo = halves(c)
        both = jnp.dot(jnp.concatenate([hi, lo], axis=0), high[m], preferred_element_type=F32)
        small = jnp.dot(hi, low[m], preferred_element_type=F32)
        return both[:frames] + (both[frames:] + small)

    receive_before(start, 0)
    receive_after(start, 0)
    coupled = product(start[...], 0) + product(before[0], 1) + product(after[0], 2)

    projected[...] = jnp.zeros_like(projected)
    number = lax.broadcasted_iota(jnp.int32, (neur_dev, LANES), 0).astype(F32)
    shift = (me * neur_dev).astype(F32)

    @pl.loop(0, n // BATCH)
    def _(b):
        hots, values = [], []
        for s in range(BATCH):
            k = b * BATCH + s
            source = origin(k)

            @pl.when(k < n - 1)
            def _():
                pltpu.make_async_remote_copy(
                    src_ref=slots.at[source], dst_ref=landed.at[source], send_sem=send_sem.at[source],
                    recv_sem=recv_sem.at[source], device_id=place(source), device_id_type=MESH).wait_recv()

        for s in range(BATCH):
            source = origin(b * BATCH + s)
            names = landed[source, frames:] - shift
            hots.append(jnp.where(number == names, 1.0, 0.0).astype(BF16))
            values.append(jnp.concatenate(halves(landed[source, :frames]), axis=0))
        projected[:, :2 * frames] += lax.dot_general(
            jnp.concatenate(hots, axis=1), jnp.concatenate(values, axis=1), NT, preferred_element_type=F32)

    sums = projected[...].T
    total = sums[:frames] + sums[frames:2 * frames]
    scale = diag[...]
    for k in range(1, SWEEPS):
        current[k - 1] = jnp.maximum((total - coupled) / scale, 0.0)
        share(current.at[k - 1], k)
        coupled = product(current[k - 1], 0)
        if k == 1:
            sent(start, 0)

            @pl.loop(0, n - 1)
            def _(i):
                slot_copy(i).wait_send()

        receive_before(current.at[k - 1], k)
        coupled = coupled + product(before[k], 1)
        receive_after(current.at[k - 1], k)
        coupled = coupled + product(after[k], 2)
    traces[...] = jnp.maximum((total - coupled) / scale, 0.0)

    for k in range(1, SWEEPS):
        sent(current.at[k - 1], k)


def local(
    movie,
    entry_tile,
    entry_neuron,
    entry_weights,
    intersection_self,
    intersection_prev,
    intersection_next,
    prev_traces,
):
    n_rows = lax.axis_size("rows")
    n = lax.axis_size("planes") * n_rows
    frames, neur_dev = prev_traces.shape
    entries = entry_tile.shape[0]
    tiles = movie.shape[0]
    cap = 2 * entries // n
    anywhere = pl.BlockSpec(memory_space=pl.ANY)
    chunks = entries // LANES
    voxels = entry_weights.shape[1]
    return pl.pallas_call(
        functools.partial(trace_kernel, n, n_rows, cap),
        in_specs=[anywhere] * 9,
        out_specs=pl.BlockSpec(memory_space=pltpu.VMEM),
        out_shape=jax.ShapeDtypeStruct((frames, neur_dev), F32),
        scratch_shapes=[
            pltpu.SMEM((entries,), jnp.int32),
            pltpu.SMEM((entries,), jnp.int32),
            pltpu.SMEM((n,), jnp.int32),
            pltpu.VMEM((chunks, LANES), jnp.int32),
            pltpu.VMEM((entries, voxels), BF16),
            pltpu.VMEM((frames, neur_dev), F32),
            pltpu.VMEM((tiles, frames * voxels), BF16),
            pltpu.VMEM((tiles, frames, LANES), F32),
            pltpu.VMEM((chunks, frames + 1, LANES), F32),
            pltpu.VMEM((n, frames + 1, LANES), F32),
            pltpu.VMEM((n, frames + 1, LANES), F32),
            pltpu.VMEM((3, neur_dev, neur_dev), F32),
            pltpu.VMEM((3, neur_dev, neur_dev), BF16),
            pltpu.VMEM((3, neur_dev, neur_dev), BF16),
            pltpu.VMEM((1, neur_dev), F32),
            pltpu.VMEM((neur_dev, LANES), F32),
            pltpu.VMEM((SWEEPS - 1, frames, neur_dev), F32),
            pltpu.VMEM((SWEEPS, frames, neur_dev), F32),
            pltpu.VMEM((SWEEPS, frames, neur_dev), F32),
            pltpu.SemaphoreType.DMA((5,)),
            pltpu.SemaphoreType.DMA((STEPS,)),
            pltpu.SemaphoreType.DMA((3,)),
            pltpu.SemaphoreType.DMA((n,)),
            pltpu.SemaphoreType.DMA((n,)),
            pltpu.SemaphoreType.DMA((2, SWEEPS)),
            pltpu.SemaphoreType.DMA((2, SWEEPS)),
        ],
        compiler_params=pltpu.CompilerParams(
            vmem_limit_bytes=60 * 2**20, collective_id=0, has_side_effects=True),
        name="traces",
    )(
        entry_tile,
        entry_neuron,
        entry_neuron.reshape(chunks, LANES),
        movie,
        entry_weights,
        intersection_self,
        intersection_prev,
        intersection_next,
        prev_traces,
    )


def solution(mesh):
    spread = ("planes", "rows")
    return jax.shard_map(
        local,
        mesh=mesh,
        in_specs=(
            P(spread, None),
            P(spread),
            P(spread),
            P(spread, None),
            P(spread, None),
            P(spread, None),
            P(spread, None),
            P(None, spread),
        ),
        out_specs=P(None, spread),
        check_vma=False,
    )
```

```python
import functools

import jax
import jax.numpy as jnp
from jax import lax
from jax.experimental import pallas as pl
from jax.experimental.pallas import tpu as pltpu
from jax.sharding import PartitionSpec as P

SWEEPS = 3
LANES = 128
STEPS = 16
BATCH = 8
ZONE = 8
F32 = jnp.float32
BF16 = jnp.bfloat16
MESH = pl.DeviceIdType.MESH
NT = (((1,), (1,)), ((), ()))


def halves(x):
    hi = x.astype(BF16)
    return hi, (x - hi.astype(F32)).astype(BF16)


def trace_kernel(
    n,
    n_rows,
    cap,
    tile_h,
    neuron_h,
    names_h,
    movie_h,
    weights_h,
    self_h,
    prev_h,
    next_h,
    start_h,
    traces,
    tile_s,
    neuron_s,
    chunk_of,
    names_v,
    weights,
    start,
    movie,
    staged,
    contrib,
    slots,
    landed,
    raw,
    high,
    low,
    diag,
    projected,
    current,
    before,
    after,
    small_sem,
    movie_sem,
    raw_sem,
    send_sem,
    recv_sem,
    near_send,
    near_recv,
):
    me = lax.axis_index("planes") * n_rows + lax.axis_index("rows")
    frames, neur_dev = start.shape

    def place(d):
        return (d // n_rows, lax.rem(d, n_rows))

    small = [
        pltpu.make_async_copy(h, v, small_sem.at[i])
        for i, (h, v) in enumerate((
            (tile_h, tile_s), (neuron_h, neuron_s), (names_h, names_v), (weights_h, weights), (start_h, start)))
    ]
    tiles = movie.shape[0]
    rows = tiles // STEPS

    def piece(i):
        part = pl.ds(pl.multiple_of(i * rows, rows), rows)
        return pltpu.make_async_copy(movie_h.at[part], movie.at[part], movie_sem.at[i])

    for i in range(STEPS):
        piece(i).start()
    for copy in small:
        copy.start()
    zones = n // ZONE
    zone, member = lax.div(me, ZONE), lax.rem(me, ZONE)

    def turn(k):
        return lax.rem(lax.div(k, ZONE) + 1, zones), lax.rem(lax.rem(k, ZONE) + 1, ZONE)

    def target(k):
        a, b = turn(k)
        return lax.rem(zone + a, zones) * ZONE + lax.rem(member + b, ZONE)

    def origin(k):
        a, b = turn(k)
        return lax.rem(zone + zones - a, zones) * ZONE + lax.rem(member + ZONE - b, ZONE)

    loads = [pltpu.make_async_copy(h, raw.at[i], raw_sem.at[i]) for i, h in enumerate((self_h, prev_h, next_h))]
    for load in loads:
        load.start()

    barrier = pltpu.get_barrier_semaphore()

    @pl.loop(1, n)
    def _(off):
        pl.semaphore_signal(barrier, inc=1, device_id=place(lax.rem(me + off, n)), device_id_type=MESH)

    flat = staged.reshape(tiles * frames, LANES)

    @pl.loop(0, STEPS)
    def _(i):
        piece(i).wait()

        @pl.loop(0, rows // 64)
        def _(r):
            for q in range(0, 64, 16):
                base = pl.multiple_of(i * rows + r * 64 + q, 16)
                for f in range(frames):
                    x = movie[pl.ds(base, 16), f * LANES:(f + 1) * LANES].astype(F32)
                    flat[pl.ds(base * frames + f, 16, stride=frames), :] = x

    for copy in small:
        copy.wait()
    lane = lax.broadcasted_iota(jnp.int32, (frames, LANES), 1)
    part = 32

    def group_of(d):
        low_end = d * neur_dev
        found = 0
        for head in range(0, tile_s.shape[0], cap):
            name = neuron_s[head]
            mine = jnp.logical_and(name >= low_end, name < low_end + neur_dev)
            found = jnp.where(mine, head // LANES, found)
        return found

    pairs = weights.shape[0] // (2 * LANES)

    @pl.loop(0, pairs)
    def _(pair):
        for j in range(n // pairs):
            d = pair * (n // pairs) + j
            chunk_of[d] = group_of(d)
        for half in range(2):
            c = pair * 2 + half
            first = pl.multiple_of(c * LANES, LANES)
            w = weights[pl.ds(first, LANES), :].astype(F32).T.astype(BF16)
            acc = jnp.zeros((frames, LANES), F32)
            for p in range(0, LANES, part):
                picked = [staged[tile_s[first + p + i]].astype(BF16) for i in range(part)]
                prod = jnp.dot(jnp.concatenate(picked, axis=0), w, preferred_element_type=F32)
                for i in range(part):
                    acc = jnp.where(lane == p + i, prod[i * frames:(i + 1) * frames], acc)
            contrib[c, :frames] = acc
            contrib[c, frames:] = names_v[pl.ds(c, 1), :].astype(F32)

    for d in range(n):
        slots[d] = contrib[chunk_of[d]]
    landed[me] = contrib[0]

    pl.semaphore_wait(barrier, n - 1)

    def to_next(src, k):
        return pltpu.make_async_remote_copy(
            src_ref=src, dst_ref=before.at[k], send_sem=near_send.at[0, k], recv_sem=near_recv.at[0, k],
            device_id=place(lax.rem(me + 1, n)), device_id_type=MESH)

    def to_prev(src, k):
        return pltpu.make_async_remote_copy(
            src_ref=src, dst_ref=after.at[k], send_sem=near_send.at[1, k], recv_sem=near_recv.at[1, k],
            device_id=place(lax.rem(me + n - 1, n)), device_id_type=MESH)

    def share(src, k):
        @pl.when(me < n - 1)
        def _():
            to_next(src, k).start()

        @pl.when(me > 0)
        def _():
            to_prev(src, k).start()

    def receive_before(src, k):
        @pl.when(me > 0)
        def _():
            to_next(src, k).wait_recv()

        @pl.when(me == 0)
        def _():
            before[k] = jnp.zeros((frames, neur_dev), F32)

    def receive_after(src, k):
        @pl.when(me < n - 1)
        def _():
            to_prev(src, k).wait_recv()

        @pl.when(me == n - 1)
        def _():
            after[k] = jnp.zeros((frames, neur_dev), F32)

    def sent(src, k):
        @pl.when(me < n - 1)
        def _():
            to_next(src, k).wait_send()

        @pl.when(me > 0)
        def _():
            to_prev(src, k).wait_send()

    share(start, 0)

    def slot_copy(k):
        d = target(k)
        return pltpu.make_async_remote_copy(
            src_ref=slots.at[d], dst_ref=landed.at[me], send_sem=send_sem.at[d], recv_sem=recv_sem.at[me],
            device_id=place(d), device_id_type=MESH)

    @pl.loop(0, n - 1)
    def _(k):
        slot_copy(k).start()

    eye = lax.broadcasted_iota(jnp.int32, (LANES, LANES), 0) == lax.broadcasted_iota(jnp.int32, (LANES, LANES), 1)
    for m in range(3):
        loads[m].wait()
        if m == 0:
            for b in range(0, neur_dev, LANES):
                block = raw[0, b:b + LANES, b:b + LANES]
                diag[:, b:b + LANES] = jnp.sum(jnp.where(eye, block, 0.0), axis=0, keepdims=True)
                raw[0, b:b + LANES, b:b + LANES] = jnp.where(eye, 0.0, block)

        @pl.loop(0, neur_dev // 64)
        def _(r):
            rows = pl.ds(pl.multiple_of(r * 64, 64), 64)
            hi, lo = halves(raw[m, rows, :])
            high[m, rows, :] = hi
            low[m, rows, :] = lo

    def product(c, m):
        hi, lo = halves(c)
        both = jnp.dot(jnp.concatenate([hi, lo], axis=0), high[m], preferred_element_type=F32)
        small = jnp.dot(hi, low[m], preferred_element_type=F32)
        return both[:frames] + (both[frames:] + small)

    receive_before(start, 0)
    receive_after(start, 0)
    coupled = product(start[...], 0) + product(before[0], 1) + product(after[0], 2)

    projected[...] = jnp.zeros_like(projected)
    number = lax.broadcasted_iota(jnp.int32, (neur_dev, LANES), 0).astype(F32)
    shift = (me * neur_dev).astype(F32)

    @pl.loop(0, n // BATCH)
    def _(b):
        hots, values = [], []
        for s in range(BATCH):
            k = b * BATCH + s
            source = origin(k)

            @pl.when(k < n - 1)
            def _():
                pltpu.make_async_remote_copy(
                    src_ref=slots.at[source], dst_ref=landed.at[source], send_sem=send_sem.at[source],
                    recv_sem=recv_sem.at[source], device_id=place(source), device_id_type=MESH).wait_recv()

        for s in range(BATCH):
            source = origin(b * BATCH + s)
            names = landed[source, frames:] - shift
            hots.append(jnp.where(number == names, 1.0, 0.0).astype(BF16))
            values.append(jnp.concatenate(halves(landed[source, :frames]), axis=0))
        projected[:, :2 * frames] += lax.dot_general(
            jnp.concatenate(hots, axis=1), jnp.concatenate(values, axis=1), NT, preferred_element_type=F32)

    sums = projected[...].T
    total = sums[:frames] + sums[frames:2 * frames]
    scale = diag[...]
    for k in range(1, SWEEPS):
        current[k - 1] = jnp.maximum((total - coupled) / scale, 0.0)
        share(current.at[k - 1], k)
        coupled = product(current[k - 1], 0)
        if k == 1:
            sent(start, 0)

            @pl.loop(0, n - 1)
            def _(i):
                slot_copy(i).wait_send()

        receive_before(current.at[k - 1], k)
        coupled = coupled + product(before[k], 1)
        receive_after(current.at[k - 1], k)
        coupled = coupled + product(after[k], 2)
    traces[...] = jnp.maximum((total - coupled) / scale, 0.0)

    for k in range(1, SWEEPS):
        sent(current.at[k - 1], k)


def local(
    movie,
    entry_tile,
    entry_neuron,
    entry_weights,
    intersection_self,
    intersection_prev,
    intersection_next,
    prev_traces,
):
    n_rows = lax.axis_size("rows")
    n = lax.axis_size("planes") * n_rows
    frames, neur_dev = prev_traces.shape
    entries = entry_tile.shape[0]
    tiles = movie.shape[0]
    cap = 2 * entries // n
    anywhere = pl.BlockSpec(memory_space=pl.ANY)
    chunks = entries // LANES
    voxels = entry_weights.shape[1]
    return pl.pallas_call(
        functools.partial(trace_kernel, n, n_rows, cap),
        in_specs=[anywhere] * 9,
        out_specs=pl.BlockSpec(memory_space=pltpu.VMEM),
        out_shape=jax.ShapeDtypeStruct((frames, neur_dev), F32),
        scratch_shapes=[
            pltpu.SMEM((entries,), jnp.int32),
            pltpu.SMEM((entries,), jnp.int32),
            pltpu.SMEM((n,), jnp.int32),
            pltpu.VMEM((chunks, LANES), jnp.int32),
            pltpu.VMEM((entries, voxels), BF16),
            pltpu.VMEM((frames, neur_dev), F32),
            pltpu.VMEM((tiles, frames * voxels), BF16),
            pltpu.VMEM((tiles, frames, LANES), F32),
            pltpu.VMEM((chunks, frames + 1, LANES), F32),
            pltpu.VMEM((n, frames + 1, LANES), F32),
            pltpu.VMEM((n, frames + 1, LANES), F32),
            pltpu.VMEM((3, neur_dev, neur_dev), F32),
            pltpu.VMEM((3, neur_dev, neur_dev), BF16),
            pltpu.VMEM((3, neur_dev, neur_dev), BF16),
            pltpu.VMEM((1, neur_dev), F32),
            pltpu.VMEM((neur_dev, LANES), F32),
            pltpu.VMEM((SWEEPS - 1, frames, neur_dev), F32),
            pltpu.VMEM((SWEEPS, frames, neur_dev), F32),
            pltpu.VMEM((SWEEPS, frames, neur_dev), F32),
            pltpu.SemaphoreType.DMA((5,)),
            pltpu.SemaphoreType.DMA((STEPS,)),
            pltpu.SemaphoreType.DMA((3,)),
            pltpu.SemaphoreType.DMA((n,)),
            pltpu.SemaphoreType.DMA((n,)),
            pltpu.SemaphoreType.DMA((2, SWEEPS)),
            pltpu.SemaphoreType.DMA((2, SWEEPS)),
        ],
        compiler_params=pltpu.CompilerParams(
            vmem_limit_bytes=60 * 2**20, collective_id=0, has_side_effects=True),
        name="traces",
    )(
        entry_tile,
        entry_neuron,
        entry_neuron.reshape(chunks, LANES),
        movie,
        entry_weights,
        intersection_self,
        intersection_prev,
        intersection_next,
        prev_traces,
    )


def solution(mesh):
    spread = ("planes", "rows")
    return jax.shard_map(
        local,
        mesh=mesh,
        in_specs=(
            P(spread, None),
            P(spread),
            P(spread),
            P(spread, None),
            P(spread, None),
            P(spread, None),
            P(spread, None),
            P(None, spread),
        ),
        out_specs=P(None, spread),
        check_vma=False,
    )
```
